128 devices in a mesh: clip: 4 (over y), tm: 4 (over z), space: 8 (over x, core).
Axes of the slice: x: 4, y: 4, z: 4, core: 2. Of those that a mesh axis runs over, the one named last changes fastest.
Arguments:
- latents: bfloat16 [8, 8, 16, 64, 384], P('clip', 'tm', 'space'), parts along dimension 0, may hold values from -6 to 6
- frame_counts: int32 [8], P('clip'), parts along dimension 0, may hold values from 1 to 8, as said below
- norm_gain: float32 [384], replicated, may hold values from 0.1 to 1.9
- norm_bias: float32 [384], replicated, may hold values from -3 to 3
- conv3_weight: bfloat16 [3, 3, 3, 384, 384], replicated, may hold values from -0.0625 to 0.0625
- conv3_bias: float32 [384], replicated, may hold values from -3 to 3
- conv2_weight: bfloat16 [3, 3, 384, 384], replicated, may hold values from -0.109375 to 0.109375
- conv2_bias: float32 [384], replicated, may hold values from -3 to 3
Outputs:
- decoded: bfloat16 [8, 8, 32, 128, 384], P('clip', 'tm', 'space'), parts along dimension 0
The draws below stay inside these ranges and needn't reach their ends.
There are 4 independent parts, one for each index of `clip`. The reference program is written for one: setup_inputs(seed, part) draws one part's arguments, and reference() takes and returns one part's arrays. A program takes and returns all parts, laid end to end along the dimension named above; an argument that names none is the same for every part. Nothing has to cross between parts.
Inputs may be any that keep to these rules, and one draw needn't show every extreme that they name: `frame_counts`: each clip has between 1 and 8 real frames; in every draw some clip has all 8.
All inputs are finite; a program needn't handle non-finite values.
Results may differ from the reference program's by a relative error of at most 0.0051.
Values may be sent and summed in bfloat16 or wider, within the bound.
A program may use at most 64 MiB of HBM per device.

```python
import jax
import jax.numpy as jnp
from jax import lax

CH = 384
GROUPS = 32
CLIPS = 2
COLS = 64
FRAMES = 8
ROWS = 16


def draw_frame_counts(key, part):
    first_key, second_key = jax.random.split(jax.random.fold_in(key, 11))
    others = jax.random.randint(first_key, (CLIPS,), 1, FRAMES)
    full_at = jax.random.randint(second_key, (), 0, CLIPS)
    clip_ids = jnp.arange(CLIPS)
    return jnp.where(clip_ids == full_at, FRAMES, others).astype(jnp.int32)


def shard_levels(rng, dims, shards, low, top_value):
    gain = 1.0
    for position, shards_of in shards:
        heights = jax.random.uniform(jax.random.fold_in(jax.random.fold_in(rng, 6), position), (shards_of,), jnp.float32, low / len(shards), top_value / len(shards))
        gain = gain * jnp.repeat(jnp.exp(heights), dims[position] // shards_of).reshape((-1,) + (1,) * (len(dims) - 1 - position))
    return gain


def normal_values(own_key, dims, spread, reach, shards=(), kind=jnp.bfloat16):
    gain = shard_levels(own_key, dims, shards, -0.22, 0.18) if shards else 1.0
    result = jax.random.normal(own_key, dims, jnp.float32) * spread * gain
    return jnp.minimum(jnp.maximum(result, -reach), reach).astype(kind)


def setup_inputs(seed: int = 0, part: int = 0) -> dict:
    key_of = jax.random.split(jax.random.key(seed), 9)
    own_keys = jax.random.split(jax.random.fold_in(key_of[8], part), 9)
    return {
        "latents": normal_values(own_keys[0], (CLIPS, FRAMES, ROWS, COLS, CH), 1.0, 6.0, ((1, 4), (2, 8))),
        "frame_counts": draw_frame_counts(jax.random.fold_in(jax.random.fold_in(key_of[8], part), 71), part),
        "norm_gain": jnp.clip(1.0 + 0.18 * jax.random.normal(key_of[2], (CH,), jnp.float32), 0.1, 1.9),
        "norm_bias": normal_values(key_of[3], (CH,), 0.5, 3.0, (), jnp.float32),
        "conv3_weight": normal_values(key_of[4], (3, 3, 3, CH, CH), (27 * CH) ** -0.5, 0.0625),
        "conv3_bias": normal_values(key_of[5], (CH,), 0.5, 3.0, (), jnp.float32),
        "conv2_weight": normal_values(key_of[6], (3, 3, CH, CH), (9 * CH) ** -0.5, 0.109375),
        "conv2_bias": normal_values(key_of[7], (CH,), 0.5, 3.0, (), jnp.float32),
    }


epsilon = 1e-05

def reference(latents, frame_counts, norm_gain, norm_bias, conv3_weight, conv3_bias, conv2_weight, conv2_bias):
    clips, frames, rows, columns, channels = latents.shape
    per_group = channels // GROUPS
    frame_ids = jnp.arange(frames, dtype=jnp.int32)
    frame_mask = (frame_ids[None, :] < frame_counts[:, None]).astype(jnp.float32)
    broad_mask = frame_mask[:, :, None, None, None]
    values = latents.astype(jnp.float32)
    grouped = (values * broad_mask).reshape(clips, frames, rows, columns, GROUPS, per_group)
    first = lax.optimization_barrier(jnp.sum(grouped, axis=(1, 2, 3, 5)))
    second = lax.optimization_barrier(jnp.sum(grouped * grouped, axis=(1, 2, 3, 5)))
    cells = (frame_counts * (rows * columns * per_group)).astype(jnp.float32)[:, None]
    mean = first / cells
    variance = second / cells - mean * mean
    scale = lax.rsqrt(variance + epsilon)
    mean_ch = jnp.repeat(mean, per_group, axis=1)[:, None, None, None, :]
    scale_ch = jnp.repeat(scale, per_group, axis=1)[:, None, None, None, :]
    activated = (jax.nn.silu((values - mean_ch) * scale_ch * norm_gain + norm_bias) * broad_mask).astype(jnp.bfloat16)
    convolved = lax.conv_general_dilated(activated.astype(jnp.float32), conv3_weight.astype(jnp.float32), (1, 1, 1), ((2, 0), (1, 1), (1, 1)), dimension_numbers=('NDHWC', 'DHWIO', 'NDHWC'), precision=lax.Precision.HIGHEST)
    middle = ((values + convolved + conv3_bias) * broad_mask).astype(jnp.bfloat16)
    upsampled = jnp.repeat(jnp.repeat(middle, 2, axis=2), 2, axis=3)
    flat = upsampled.reshape(clips * frames, 2 * rows, 2 * columns, channels).astype(jnp.float32)
    planar = lax.conv_general_dilated(flat, conv2_weight.astype(jnp.float32), (1, 1), ((1, 1), (1, 1)), dimension_numbers=('NHWC', 'HWIO', 'NHWC'), precision=lax.Precision.HIGHEST)
    planar = planar.reshape(clips, frames, 2 * rows, 2 * columns, channels)
    return ((planar + conv2_bias) * broad_mask).astype(jnp.bfloat16)
```

```python
import functools

import jax
import jax.numpy as jnp
from jax import lax
from jax.experimental import pallas as pl
from jax.experimental.pallas import tpu as pltpu
from jax.sharding import PartitionSpec as P

MESH = pl.DeviceIdType.MESH
EPS = 1e-05
CH = 384
GROUP = 12
COLS = 64
F32 = jnp.float32
BF16 = jnp.bfloat16
UNITS = ((0, 1), (0, 0), (1, 1), (1, 0))


def dot(a, b):
    return jnp.dot(a, b, preferred_element_type=F32)


def exact_dot(a, b):
    return jnp.dot(a, b, preferred_element_type=F32, precision=lax.Precision.HIGHEST)


def kernel(
    cells, lat, counts, gain, nbias, w3, b3, w2, b2, out,
    x, act, wide, raw2, phase, acc, mid, gath_t, gath_s, inter, coef,
    lsem, wsem, w2sem, ts_s, ts_r, ss_s, ss_r, z_s, z_r, h_s, h_r, c_s, c_r, m_s, m_r,
):
    n_t, n_s = lax.axis_size("tm"), lax.axis_size("space")
    t_me, s_me = lax.axis_index("tm"), lax.axis_index("space")
    along_t = lambda d: {"tm": lax.rem(t_me + d, n_t)}
    along_s = lambda d: {"space": lax.rem(s_me + d, n_s)}
    up, down = along_s(n_s - 1), along_s(1)

    def remote(src, dst, send, recv, device):
        return pltpu.make_async_remote_copy(
            src_ref=src, dst_ref=dst, send_sem=send, recv_sem=recv, device_id=device, device_id_type=MESH
        )

    own = pltpu.make_async_copy(lat, x.at[:, pl.ds(2, 2), pl.ds(1, 2)], lsem)
    own.start()
    w2_copy = pltpu.make_async_copy(w2, raw2, w2sem)
    w2_copy.start()
    w3_copies = [
        pltpu.make_async_copy(w3.at[a, :, e], wide.at[a, :, :, pl.ds(e * CH, CH)], wsem.at[a * 3 + e])
        for a in (2, 1, 0)
        for e in range(3)
    ]
    for copy in w3_copies:
        copy.start()

    barrier = pltpu.get_barrier_semaphore()
    peers = [along_t(d) for d in range(1, n_t)] + [along_s(d) for d in range(1, n_s)]
    for peer in peers:
        pl.semaphore_signal(barrier, inc=1, device_id=peer, device_id_type=MESH)

    def present(c, frame):
        return (frame < counts[c]).astype(F32)

    own.wait()
    firsts, seconds = [], []
    for c in range(2):
        first = jnp.zeros((8, CH), F32)
        second = jnp.zeros((8, CH), F32)
        for f in range(2):
            f1 = jnp.zeros((8, CH), F32)
            f2 = jnp.zeros((8, CH), F32)
            for r in range(2):
                v = x[c, 2 + f, 1 + r].astype(F32).reshape(8, 8, CH)
                f1 += jnp.sum(v, axis=0)
                f2 += jnp.sum(v * v, axis=0)
            there = present(c, 2 * t_me + f)
            first += f1 * there
            second += f2 * there
        firsts.append(jnp.sum(first, axis=0, keepdims=True))
        seconds.append(jnp.sum(second, axis=0, keepdims=True))
    sums = jnp.concatenate(firsts + seconds + [jnp.zeros((4, CH), F32)], axis=0)
    channel = lax.broadcasted_iota(jnp.int32, (CH, 128), 0)
    low = lax.broadcasted_iota(jnp.int32, (CH, 128), 1) * GROUP
    member = jnp.where((channel >= low) & (channel < low + GROUP), 1.0, 0.0).astype(F32)
    gath_t[0] = exact_dot(sums, member)

    pl.semaphore_wait(barrier, len(peers))

    stat_t = [remote(gath_t.at[0], gath_t.at[d], ts_s.at[d], ts_r.at[d], along_t(d)) for d in range(1, n_t)]
    for copy in stat_t:
        copy.start()
    z_copies = {
        (c, f): remote(lat.at[c, f], x.at[c, f, pl.ds(1, 2)], z_s.at[c * 2 + f], z_r.at[c * 2 + f], along_t(1))
        for c, f in UNITS
    }

    @pl.when(t_me < n_t - 1)
    def _():
        for unit in UNITS:
            z_copies[unit].start()

    halo = []
    for c in range(2):
        halo.append((
            remote(lat.at[c, :, 1], x.at[c, pl.ds(2, 2), 0], h_s.at[2 * c], h_r.at[2 * c], down),
            remote(lat.at[c, :, 0], x.at[c, pl.ds(2, 2), 3], h_s.at[2 * c + 1], h_r.at[2 * c + 1], up),
        ))
    for pair in halo:
        for copy in pair:
            copy.start()

    w2_copy.wait()

    def fold(i, carry):
        rows = pl.ds(pl.multiple_of(i * 64, 64), 64)
        by_row = [[raw2[b, e, rows].astype(F32) for e in range(3)] for b in range(3)]
        for p, u, picks in ((0, 0, (0,)), (0, 1, (1, 2)), (1, 0, (0, 1)), (1, 1, (2,))):
            taps = [functools.reduce(jnp.add, [by_row[b][e] for b in picks]) for e in range(3)]
            phase[p, u, rows, 0:CH] = taps[0].astype(BF16)
            phase[p, u, rows, CH : 2 * CH] = (taps[0] + taps[1] + taps[2]).astype(BF16)
            phase[p, u, rows, 2 * CH : 3 * CH] = taps[2].astype(BF16)
        return carry

    lax.fori_loop(0, CH // 64, fold, 0)

    for copy in stat_t:
        copy.wait_recv()
    gath_s[0] = gath_t[0] + gath_t[1] + gath_t[2] + gath_t[3]
    stat_s = [remote(gath_s.at[0], gath_s.at[d], ss_s.at[d], ss_r.at[d], along_s(d)) for d in range(1, n_s)]
    for copy in stat_s:
        copy.start()

    corner = {
        (c, f): (
            remote(x.at[c, f, 2], x.at[c, f, 0], c_s.at[c * 4 + f * 2], c_r.at[c * 4 + f * 2], down),
            remote(x.at[c, f, 1], x.at[c, f, 3], c_s.at[c * 4 + f * 2 + 1], c_r.at[c * 4 + f * 2 + 1], up),
        )
        for c, f in UNITS
    }

    def forward(unit):
        @pl.when(t_me > 0)
        def _():
            z_copies[unit].wait_recv()
            for copy in corner[unit]:
                copy.start()

    forward(UNITS[0])

    for copy in stat_s:
        copy.wait_recv()
    total = gath_s[0]
    for d in range(1, n_s):
        total = total + gath_s[d]
    means, scales = [], []
    for c in range(2):
        number = (counts[c] * (cells * GROUP)).astype(F32)
        mean = total[c : c + 1] / number
        variance = total[2 + c : 3 + c] / number - mean * mean
        means.append(mean)
        scales.append(lax.rsqrt(variance + EPS))
    packed = jnp.concatenate(means + scales + [jnp.zeros((4, 128), F32)], axis=0)
    group = lax.broadcasted_iota(jnp.int32, (128, CH), 0) * GROUP
    channel = lax.broadcasted_iota(jnp.int32, (128, CH), 1)
    spread = jnp.where((channel >= group) & (channel < group + GROUP), 1.0, 0.0).astype(F32)
    coef[...] = exact_dot(packed, spread)

    def activate(c, f):
        there = present(c, 2 * t_me - 2 + f)

        def row(r, carry):
            inside = jnp.where(((r == 0) & (s_me == 0)) | ((r == 3) & (s_me == n_s - 1)), 0.0, there)
            half = (x[c, f, r].astype(F32) - coef[c : c + 1]) * (coef[2 + c : 3 + c] * gain[...] * 0.5) + nbias[...] * 0.5
            act[c, f, r] = ((half + half * jnp.tanh(half)) * inside).astype(BF16)
            return carry

        lax.fori_loop(0, 4, row, 0)

    column = lax.rem(lax.broadcasted_iota(jnp.int32, (2 * COLS, CH), 0), COLS)
    not_first, not_last = column > 0, column < COLS - 1

    def before(v):
        return jnp.where(not_first, pltpu.roll(v, 1, 0), 0.0)

    def after(v):
        return jnp.where(not_last, pltpu.roll(v, 2 * COLS - 1, 0), 0.0)

    def volume(c, frames, taps):
        lhs = jnp.concatenate(
            [jnp.concatenate([act[c, f, r + b] for f in frames for b in range(3)], axis=1) for r in range(2)], axis=0
        )
        rhs = wide[pl.ds(taps[0], len(taps))].reshape(len(taps) * 3 * CH, 3 * CH)
        prod = dot(lhs, rhs)
        return before(prod[:, 0:CH]) + prod[:, CH : 2 * CH] + after(prod[:, 2 * CH :])

    def own_part(c):
        acc[c, 0] = volume(c, (2,), (2,))
        acc[c, 1] = volume(c, (2, 3), (1, 2))

    def finish(c):
        for f in range(2):
            kept = present(c, 2 * t_me + f)
            resid = jnp.concatenate([x[c, 2 + f, 1], x[c, 2 + f, 2]], axis=0).astype(F32)
            value = ((resid + acc[c, f] + b3[...]) * kept).astype(BF16)
            mid[c, f, 1] = value[:COLS]
            mid[c, f, 2] = value[COLS:]

    mid_copies = [
        (
            remote(mid.at[c, :, 2], mid.at[c, :, 0], m_s.at[2 * c], m_r.at[2 * c], down),
            remote(mid.at[c, :, 1], mid.at[c, :, 3], m_s.at[2 * c + 1], m_r.at[2 * c + 1], up),
        )
        for c in range(2)
    ]

    def emit(c, p, r, first_row):
        lhs = jnp.concatenate([jnp.concatenate([mid[c, f, first_row], mid[c, f, first_row + 1]], axis=1) for f in range(2)], axis=0)
        prod = dot(lhs, phase[p].reshape(2 * CH, 3 * CH))
        left, centre, right = prod[:, 0:CH], prod[:, CH : 2 * CH], prod[:, 2 * CH :]
        centre = centre + b2[...]
        even = centre + (before(left) - left)
        odd = centre + (after(right) - right)
        for f in range(2):
            kept = present(c, 2 * t_me + f)
            for lane in range(CH // 128):
                cut = slice(lane * 128, lane * 128 + 128)
                rows = slice(f * COLS, (f + 1) * COLS)
                inter[f, lane, pl.ds(0, COLS, stride=2)] = even[rows, cut] * kept
                inter[f, lane, pl.ds(1, COLS, stride=2)] = odd[rows, cut] * kept
                out[c, f, 2 * r + p, :, cut] = inter[f, lane].astype(BF16)

    def inner(c):
        emit(c, 1, 0, 1)
        emit(c, 0, 1, 1)

    def outer(c):
        for copy in mid_copies[c]:
            copy.wait_recv()

        @pl.when(s_me == 0)
        def _():
            mid[c, :, 0] = jnp.zeros((2, COLS, CH), BF16)

        @pl.when(s_me == n_s - 1)
        def _():
            mid[c, :, 3] = jnp.zeros((2, COLS, CH), BF16)

        emit(c, 0, 0, 0)
        emit(c, 1, 1, 2)

    def arrived(unit):
        for copy in corner[unit]:
            copy.wait_recv()

    for copy in halo[0]:
        copy.wait_recv()
    activate(0, 2)
    activate(0, 3)
    forward(UNITS[1])
    for copy in w3_copies:
        copy.wait()
    own_part(0)
    for copy in halo[1]:
        copy.wait_recv()
    activate(1, 2)
    activate(1, 3)
    forward(UNITS[2])
    own_part(1)
    forward(UNITS[3])

    @pl.when(t_me > 0)
    def _():
        arrived((0, 1))
        activate(0, 1)
        arrived((0, 0))
        activate(0, 0)
        acc[0, 1] += volume(0, (1,), (0,))
        acc[0, 0] += volume(0, (0, 1), (0, 1))

    finish(0)
    for copy in mid_copies[0]:
        copy.start()

    @pl.when(t_me > 0)
    def _():
        arrived((1, 1))
        activate(1, 1)
        acc[1, 1] += volume(1, (1,), (0,))
        acc[1, 0] += volume(1, (1,), (1,))
        arrived((1, 0))
        activate(1, 0)
        acc[1, 0] += volume(1, (0,), (0,))

    finish(1)
    for copy in mid_copies[1]:
        copy.start()

    inner(0)
    outer(0)
    inner(1)
    outer(1)

    for copy in stat_t + stat_s + [copy for pair in halo + mid_copies for copy in pair]:
        copy.wait_send()

    @pl.when(t_me < n_t - 1)
    def _():
        for unit in UNITS:
            z_copies[unit].wait_send()

    @pl.when(t_me > 0)
    def _():
        for unit in UNITS:
            for copy in corner[unit]:
                copy.wait_send()


def body(latents, frame_counts, norm_gain, norm_bias, conv3_weight, conv3_bias, conv2_weight, conv2_bias):
    rows = latents.shape[2] * lax.axis_size("space")
    row = lambda v: v.reshape(1, CH)
    hbm, vmem, smem = (pl.BlockSpec(memory_space=space) for space in (pl.ANY, pltpu.VMEM, pltpu.SMEM))
    dma = pltpu.SemaphoreType.DMA
    return pl.pallas_call(
        functools.partial(kernel, rows * COLS),
        out_shape=jax.ShapeDtypeStruct((2, 2, 4, 2 * COLS, CH), BF16),
        in_specs=[hbm, smem, vmem, vmem, hbm, vmem, hbm, vmem],
        out_specs=vmem,
        scratch_shapes=[
            pltpu.VMEM((2, 4, 4, COLS, CH), BF16),
            pltpu.VMEM((2, 4, 4, COLS, CH), BF16),
            pltpu.VMEM((3, 3, CH, 3 * CH), BF16),
            pltpu.VMEM((3, 3, CH, CH), BF16),
            pltpu.VMEM((2, 2, CH, 3 * CH), BF16),
            pltpu.VMEM((2, 2, 2 * COLS, CH), F32),
            pltpu.VMEM((2, 2, 4, COLS, CH), BF16),
            pltpu.VMEM((4, 8, 128), F32),
            pltpu.VMEM((8, 8, 128), F32),
            pltpu.VMEM((2, 3, 2 * COLS, 128), F32),
            pltpu.VMEM((8, CH), F32),
            dma, dma((9,)), dma, dma((4,)), dma((4,)), dma((8,)), dma((8,)),
            dma((4,)), dma((4,)), dma((4,)), dma((4,)), dma((8,)), dma((8,)), dma((4,)), dma((4,)),
        ],
        compiler_params=pltpu.CompilerParams(collective_id=0, has_side_effects=True, vmem_limit_bytes=58 * 2**20),
        cost_estimate=pl.CostEstimate(flops=7 * 10**9, bytes_accessed=13 * 10**6, transcendentals=10**6),
    )(latents, frame_counts, row(norm_gain), row(norm_bias), conv3_weight, row(conv3_bias), conv2_weight, row(conv2_bias))


def solution(mesh):
    placed = (P("clip", "tm", "space", None, None), P("clip"), P(), P(), P(), P(), P(), P())
    return jax.shard_map(
        body, mesh=mesh, in_specs=placed, out_specs=P("clip", "tm", "space", None, None), check_vma=False
    )
```

```python
import functools

import jax
import jax.numpy as jnp
from jax import lax
from jax.experimental import pallas as pl
from jax.experimental.pallas import tpu as pltpu
from jax.sharding import PartitionSpec as P

MESH = pl.DeviceIdType.MESH
EPS = 1e-05
CH = 384
GROUP = 12
COLS = 64
F32 = jnp.float32
BF16 = jnp.bfloat16
UNITS = ((0, 1), (0, 0), (1, 1), (1, 0))


def dot(a, b):
    return jnp.dot(a, b, preferred_element_type=F32)


def exact_dot(a, b):
    return jnp.dot(a, b, preferred_element_type=F32, precision=lax.Precision.HIGHEST)


def kernel(
    cells, lat, counts, gain, nbias, w3, b3, w2, b2, out,
    x, act, wide, raw2, phase, acc, mid, gath_t, gath_s, inter, coef,
    lsem, wsem, w2sem, ts_s, ts_r, ss_s, ss_r, z_s, z_r, h_s, h_r, c_s, c_r, m_s, m_r,
):
    n_t, n_s = lax.axis_size("tm"), lax.axis_size("space")
    t_me, s_me = lax.axis_index("tm"), lax.axis_index("space")
    along_t = lambda d: {"tm": lax.rem(t_me + d, n_t)}
    along_s = lambda d: {"space": lax.rem(s_me + d, n_s)}
    up, down = along_s(n_s - 1), along_s(1)

    def remote(src, dst, send, recv, device):
        return pltpu.make_async_remote_copy(
            src_ref=src, dst_ref=dst, send_sem=send, recv_sem=recv, device_id=device, device_id_type=MESH
        )

    own = pltpu.make_async_copy(lat, x.at[:, pl.ds(2, 2), pl.ds(1, 2)], lsem)
    own.start()
    w2_copy = pltpu.make_async_copy(w2, raw2, w2sem)
    w2_copy.start()
    w3_copies = [
        pltpu.make_async_copy(w3.at[a, :, e], wide.at[a, :, :, pl.ds(e * CH, CH)], wsem.at[a * 3 + e])
        for a in (2, 1, 0)
        for e in range(3)
    ]
    for copy in w3_copies:
        copy.start()

    barrier = pltpu.get_barrier_semaphore()
    peers = [along_t(d) for d in range(1, n_t)] + [along_s(d) for d in range(1, n_s)]
    for peer in peers:
        pl.semaphore_signal(barrier, inc=1, device_id=peer, device_id_type=MESH)

    def present(c, frame):
        return (frame < counts[c]).astype(F32)

    own.wait()
    firsts, seconds = [], []
    for c in range(2):
        first = jnp.zeros((8, CH), F32)
        second = jnp.zeros((8, CH), F32)
        for f in range(2):
            f1 = jnp.zeros((8, CH), F32)
            f2 = jnp.zeros((8, CH), F32)
            for r in range(2):
                v = x[c, 2 + f, 1 + r].astype(F32).reshape(8, 8, CH)
                f1 += jnp.sum(v, axis=0)
                f2 += jnp.sum(v * v, axis=0)
            there = present(c, 2 * t_me + f)
            first += f1 * there
            second += f2 * there
        firsts.append(jnp.sum(first, axis=0, keepdims=True))
        seconds.append(jnp.sum(second, axis=0, keepdims=True))
    sums = jnp.concatenate(firsts + seconds + [jnp.zeros((4, CH), F32)], axis=0)
    channel = lax.broadcasted_iota(jnp.int32, (CH, 128), 0)
    low = lax.broadcasted_iota(jnp.int32, (CH, 128), 1) * GROUP
    member = jnp.where((channel >= low) & (channel < low + GROUP), 1.0, 0.0).astype(F32)
    gath_t[0] = exact_dot(sums, member)

    pl.semaphore_wait(barrier, len(peers))

    stat_t = [remote(gath_t.at[0], gath_t.at[d], ts_s.at[d], ts_r.at[d], along_t(d)) for d in range(1, n_t)]
    for copy in stat_t:
        copy.start()
    z_copies = {
        (c, f): remote(lat.at[c, f], x.at[c, f, pl.ds(1, 2)], z_s.at[c * 2 + f], z_r.at[c * 2 + f], along_t(1))
        for c, f in UNITS
    }

    @pl.when(t_me < n_t - 1)
    def _():
        for unit in UNITS:
            z_copies[unit].start()

    halo = []
    for c in range(2):
        halo.append((
            remote(lat.at[c, :, 1], x.at[c, pl.ds(2, 2), 0], h_s.at[2 * c], h_r.at[2 * c], down),
            remote(lat.at[c, :, 0], x.at[c, pl.ds(2, 2), 3], h_s.at[2 * c + 1], h_r.at[2 * c + 1], up),
        ))
    for pair in halo:
        for copy in pair:
            copy.start()

    w2_copy.wait()

    def fold(i, carry):
        rows = pl.ds(pl.multiple_of(i * 64, 64), 64)
        by_row = [[raw2[b, e, rows].astype(F32) for e in range(3)] for b in range(3)]
        for p, u, picks in ((0, 0, (0,)), (0, 1, (1, 2)), (1, 0, (0, 1)), (1, 1, (2,))):
            taps = [functools.reduce(jnp.add, [by_row[b][e] for b in picks]) for e in range(3)]
            phase[p, u, rows, 0:CH] = taps[0].astype(BF16)
            phase[p, u, rows, CH : 2 * CH] = (taps[0] + taps[1] + taps[2]).astype(BF16)
            phase[p, u, rows, 2 * CH : 3 * CH] = taps[2].astype(BF16)
        return carry

    lax.fori_loop(0, CH // 64, fold, 0)

    for copy in stat_t:
        copy.wait_recv()
    gath_s[0] = gath_t[0] + gath_t[1] + gath_t[2] + gath_t[3]
    stat_s = [remote(gath_s.at[0], gath_s.at[d], ss_s.at[d], ss_r.at[d], along_s(d)) for d in range(1, n_s)]
    for copy in stat_s:
        copy.start()

    corner = {
        (c, f): (
            remote(x.at[c, f, 2], x.at[c, f, 0], c_s.at[c * 4 + f * 2], c_r.at[c * 4 + f * 2], down),
            remote(x.at[c, f, 1], x.at[c, f, 3], c_s.at[c * 4 + f * 2 + 1], c_r.at[c * 4 + f * 2 + 1], up),
        )
        for c, f in UNITS
    }

    def forward(unit):
        @pl.when(t_me > 0)
        def _():
            z_copies[unit].wait_recv()
            for copy in corner[unit]:
                copy.start()

    forward(UNITS[0])

    for copy in stat_s:
        copy.wait_recv()
    total = gath_s[0]
    for d in range(1, n_s):
        total = total + gath_s[d]
    means, scales = [], []
    for c in range(2):
        number = (counts[c] * (cells * GROUP)).astype(F32)
        mean = total[c : c + 1] / number
        variance = total[2 + c : 3 + c] / number - mean * mean
        means.append(mean)
        scales.append(lax.rsqrt(variance + EPS))
    packed = jnp.concatenate(means + scales + [jnp.zeros((4, 128), F32)], axis=0)
    group = lax.broadcasted_iota(jnp.int32, (128, CH), 0) * GROUP
    channel = lax.broadcasted_iota(jnp.int32, (128, CH), 1)
    spread = jnp.where((channel >= group) & (channel < group + GROUP), 1.0, 0.0).astype(F32)
    coef[...] = exact_dot(packed, spread)

    def activate(c, f):
        there = present(c, 2 * t_me - 2 + f)

        def row(r, carry):
            inside = jnp.where(((r == 0) & (s_me == 0)) | ((r == 3) & (s_me == n_s - 1)), 0.0, there)
            half = (x[c, f, r].astype(F32) - coef[c : c + 1]) * (coef[2 + c : 3 + c] * gain[...].reshape(1, CH) * 0.5) + nbias[...].reshape(1, CH) * 0.5
            act[c, f, r] = ((half + half * jnp.tanh(half)) * inside).astype(BF16)
            return carry

        lax.fori_loop(0, 4, row, 0)

    column = lax.rem(lax.broadcasted_iota(jnp.int32, (2 * COLS, CH), 0), COLS)
    not_first, not_last = column > 0, column < COLS - 1

    def before(v):
        return jnp.where(not_first, pltpu.roll(v, 1, 0), 0.0)

    def after(v):
        return jnp.where(not_last, pltpu.roll(v, 2 * COLS - 1, 0), 0.0)

    def volume(c, frames, taps):
        lhs = jnp.concatenate(
            [jnp.concatenate([act[c, f, r + b] for f in frames for b in range(3)], axis=1) for r in range(2)], axis=0
        )
        rhs = wide[pl.ds(taps[0], len(taps))].reshape(len(taps) * 3 * CH, 3 * CH)
        prod = dot(lhs, rhs)
        return before(prod[:, 0:CH]) + prod[:, CH : 2 * CH] + after(prod[:, 2 * CH :])

    def own_part(c):
        acc[c, 0] = volume(c, (2,), (2,))
        acc[c, 1] = volume(c, (2, 3), (1, 2))

    def finish(c):
        for f in range(2):
            kept = present(c, 2 * t_me + f)
            resid = jnp.concatenate([x[c, 2 + f, 1], x[c, 2 + f, 2]], axis=0).astype(F32)
            value = ((resid + acc[c, f] + b3[...].reshape(1, CH)) * kept).astype(BF16)
            mid[c, f, 1] = value[:COLS]
            mid[c, f, 2] = value[COLS:]

    mid_copies = [
        (
            remote(mid.at[c, :, 2], mid.at[c, :, 0], m_s.at[2 * c], m_r.at[2 * c], down),
            remote(mid.at[c, :, 1], mid.at[c, :, 3], m_s.at[2 * c + 1], m_r.at[2 * c + 1], up),
        )
        for c in range(2)
    ]

    def emit(c, p, r, first_row):
        lhs = jnp.concatenate([jnp.concatenate([mid[c, f, first_row], mid[c, f, first_row + 1]], axis=1) for f in range(2)], axis=0)
        prod = dot(lhs, phase[p].reshape(2 * CH, 3 * CH))
        left, centre, right = prod[:, 0:CH], prod[:, CH : 2 * CH], prod[:, 2 * CH :]
        centre = centre + b2[...].reshape(1, CH)
        even = centre + (before(left) - left)
        odd = centre + (after(right) - right)
        for f in range(2):
            kept = present(c, 2 * t_me + f)
            for lane in range(CH // 128):
                cut = slice(lane * 128, lane * 128 + 128)
                rows = slice(f * COLS, (f + 1) * COLS)
                inter[f, lane, pl.ds(0, COLS, stride=2)] = even[rows, cut] * kept
                inter[f, lane, pl.ds(1, COLS, stride=2)] = odd[rows, cut] * kept
                out[c, f, 2 * r + p, :, cut] = inter[f, lane].astype(BF16)

    def inner(c):
        emit(c, 1, 0, 1)
        emit(c, 0, 1, 1)

    def outer(c):
        for copy in mid_copies[c]:
            copy.wait_recv()

        @pl.when(s_me == 0)
        def _():
            mid[c, :, 0] = jnp.zeros((2, COLS, CH), BF16)

        @pl.when(s_me == n_s - 1)
        def _():
            mid[c, :, 3] = jnp.zeros((2, COLS, CH), BF16)

        emit(c, 0, 0, 0)
        emit(c, 1, 1, 2)

    def arrived(unit):
        for copy in corner[unit]:
            copy.wait_recv()

    for copy in halo[0]:
        copy.wait_recv()
    activate(0, 2)
    activate(0, 3)
    forward(UNITS[1])
    for copy in w3_copies:
        copy.wait()
    own_part(0)
    for copy in halo[1]:
        copy.wait_recv()
    activate(1, 2)
    activate(1, 3)
    forward(UNITS[2])
    own_part(1)
    forward(UNITS[3])

    @pl.when(t_me > 0)
    def _():
        arrived((0, 1))
        activate(0, 1)
        arrived((0, 0))
        activate(0, 0)
        acc[0, 1] += volume(0, (1,), (0,))
        acc[0, 0] += volume(0, (0, 1), (0, 1))

    finish(0)
    for copy in mid_copies[0]:
        copy.start()

    @pl.when(t_me > 0)
    def _():
        arrived((1, 1))
        activate(1, 1)
        acc[1, 1] += volume(1, (1,), (0,))
        acc[1, 0] += volume(1, (1,), (1,))
        arrived((1, 0))
        activate(1, 0)
        acc[1, 0] += volume(1, (0,), (0,))

    finish(1)
    for copy in mid_copies[1]:
        copy.start()

    inner(0)
    outer(0)
    inner(1)
    outer(1)

    for copy in stat_t + stat_s + [copy for pair in halo + mid_copies for copy in pair]:
        copy.wait_send()

    @pl.when(t_me < n_t - 1)
    def _():
        for unit in UNITS:
            z_copies[unit].wait_send()

    @pl.when(t_me > 0)
    def _():
        for unit in UNITS:
            for copy in corner[unit]:
                copy.wait_send()


def body(latents, frame_counts, norm_gain, norm_bias, conv3_weight, conv3_bias, conv2_weight, conv2_bias):
    rows = latents.shape[2] * lax.axis_size("space")
    hbm, vmem, smem = (pl.BlockSpec(memory_space=space) for space in (pltpu.HBM, pltpu.VMEM, pltpu.SMEM))
    dma = pltpu.SemaphoreType.DMA
    return pl.pallas_call(
        functools.partial(kernel, rows * COLS),
        out_shape=jax.ShapeDtypeStruct((2, 2, 4, 2 * COLS, CH), BF16),
        in_specs=[hbm, smem, vmem, vmem, hbm, vmem, hbm, vmem],
        out_specs=vmem,
        scratch_shapes=[
            pltpu.VMEM((2, 4, 4, COLS, CH), BF16),
            pltpu.VMEM((2, 4, 4, COLS, CH), BF16),
            pltpu.VMEM((3, 3, CH, 3 * CH), BF16),
            pltpu.VMEM((3, 3, CH, CH), BF16),
            pltpu.VMEM((2, 2, CH, 3 * CH), BF16),
            pltpu.VMEM((2, 2, 2 * COLS, CH), F32),
            pltpu.VMEM((2, 2, 4, COLS, CH), BF16),
            pltpu.VMEM((4, 8, 128), F32),
            pltpu.VMEM((8, 8, 128), F32),
            pltpu.VMEM((2, 3, 2 * COLS, 128), F32),
            pltpu.VMEM((8, CH), F32),
            dma, dma((9,)), dma, dma((4,)), dma((4,)), dma((8,)), dma((8,)),
            dma((4,)), dma((4,)), dma((4,)), dma((4,)), dma((8,)), dma((8,)), dma((4,)), dma((4,)),
        ],
        compiler_params=pltpu.CompilerParams(collective_id=0, has_side_effects=True, vmem_limit_bytes=58 * 2**20),
        cost_estimate=pl.CostEstimate(flops=7 * 10**9, bytes_accessed=13 * 10**6, transcendentals=10**6),
    )(latents, frame_counts, norm_gain, norm_bias, conv3_weight, conv3_bias, conv2_weight, conv2_bias)


def solution(mesh):
    placed = (P("clip", "tm", "space", None, None), P("clip"), P(), P(), P(), P(), P(), P())
    return jax.shard_map(
        body, mesh=mesh, in_specs=placed, out_specs=P("clip", "tm", "space", None, None), check_vma=False
    )
```

```python
import functools

import jax
import jax.numpy as jnp
from jax import lax
from jax.experimental import pallas as pl
from jax.experimental.pallas import tpu as pltpu
from jax.sharding import PartitionSpec as P

MESH = pl.DeviceIdType.MESH
EPS = 1e-05
CH = 384
GROUP = 12
COLS = 64
F32 = jnp.float32
BF16 = jnp.bfloat16
UNITS = ((0, 1), (0, 0), (1, 1), (1, 0))


def dot(a, b):
    return jnp.dot(a, b, preferred_element_type=F32)


def exact_dot(a, onehot):
    high = a.astype(BF16)
    rest = a - high.astype(F32)
    middle = rest.astype(BF16)
    low = (rest - middle.astype(F32)).astype(BF16)
    parts = dot(jnp.concatenate([high.astype(F32), middle.astype(F32), low.astype(F32)], axis=0).astype(BF16), onehot)
    return parts[0:8] + parts[8:16] + parts[16:24]


def membership(shape, channel_axis):
    channel = lax.broadcasted_iota(jnp.int32, shape, channel_axis)
    first = lax.rem(lax.broadcasted_iota(jnp.int32, shape, 1 - channel_axis), 32) * GROUP
    return jnp.where((channel >= first) & (channel < first + GROUP), 1.0, 0.0).astype(BF16)


def kernel(
    cells, lat, counts, gain, nbias, w3, b3, w2, b2, out,
    x, act, wide, raw2, phase, acc, mid, pair, gath, inter, coef, ready, last,
    lsem, wsem, w2sem, p_s, p_r, g_s, g_r, z_s, z_r, h_s, h_r, c_s, c_r, m_s, m_r, o_s,
):
    n_t, n_s = lax.axis_size("tm"), lax.axis_size("space")
    t_me, s_me = lax.axis_index("tm"), lax.axis_index("space")
    later = {"tm": lax.rem(t_me + 1, n_t)}
    up, down = {"space": lax.rem(s_me + n_s - 1, n_s)}, {"space": lax.rem(s_me + 1, n_s)}

    def remote(src, dst, send, recv, device):
        return pltpu.make_async_remote_copy(
            src_ref=src, dst_ref=dst, send_sem=send, recv_sem=recv, device_id=device, device_id_type=MESH
        )

    own = pltpu.make_async_copy(lat, x.at[:, pl.ds(2, 2), pl.ds(2, 2)], lsem)
    own.start()

    column_peers = [{"tm": lax.rem(t_me + d, n_t)} for d in range(n_t)]
    row_peers = [{"space": lax.rem(s_me + d, n_s)} for d in range(n_s)]
    peers = column_peers[1:] + row_peers[1:]
    barrier = pltpu.get_barrier_semaphore()
    for peer in peers:
        pl.semaphore_signal(barrier, inc=1, device_id=peer, device_id_type=MESH)

    w2_copy = pltpu.make_async_copy(w2, raw2, w2sem)
    w2_copy.start()
    w3_copies = [
        pltpu.make_async_copy(w3.at[a, :, e], wide.at[a, :, :, pl.ds(e * CH, CH)], wsem.at[a * 3 + e])
        for a in (2, 1, 0)
        for e in range(3)
    ]
    for copy in w3_copies:
        copy.start()

    def present(c, frame):
        return (frame < counts[c]).astype(F32)

    own.wait()
    firsts, seconds = [], []
    for c in range(2):
        first = jnp.zeros((8, CH), F32)
        second = jnp.zeros((8, CH), F32)
        for f in range(2):
            f1 = jnp.zeros((8, CH), F32)
            f2 = jnp.zeros((8, CH), F32)
            for r in range(2):
                v = x[c, 2 + f, 2 + r].astype(F32).reshape(8, 8, CH)
                f1 += jnp.sum(v, axis=0)
                f2 += jnp.sum(v * v, axis=0)
            there = present(c, 2 * t_me + f)
            first += f1 * there
            second += f2 * there
        firsts.append(jnp.sum(first, axis=0, keepdims=True))
        seconds.append(jnp.sum(second, axis=0, keepdims=True))
    sums = jnp.concatenate(firsts + seconds + [jnp.zeros((4, CH), F32)], axis=0)
    grouped = exact_dot(sums, membership((CH, 128), 0))
    lane_row = lax.broadcasted_iota(jnp.int32, (8, 128), 1) // 32
    diagonal = lane_row == lax.broadcasted_iota(jnp.int32, (8, 128), 0)
    gath[0] = jnp.sum(jnp.where(diagonal, grouped, 0.0), axis=0, keepdims=True)

    pl.semaphore_wait(barrier, len(peers))

    sums_a = [remote(gath.at[0], gath.at[d], g_s.at[d], g_r.at[d], column_peers[d]) for d in range(1, n_t)]
    for copy in sums_a:
        copy.start()
    z_copies = {
        (c, f): remote(lat.at[c, f], x.at[c, f, pl.ds(2, 2)], z_s.at[c * 2 + f], z_r.at[c * 2 + f], later)
        for c, f in UNITS
    }

    @pl.when(t_me < n_t - 1)
    def _():
        for unit in UNITS:
            z_copies[unit].start()

    halo = []
    for c in range(2):
        halo.append((
            remote(lat.at[c, :, 1], x.at[c, pl.ds(2, 2), 1], h_s.at[2 * c], h_r.at[2 * c], down),
            remote(lat.at[c, :, 0], x.at[c, pl.ds(2, 2), 4], h_s.at[2 * c + 1], h_r.at[2 * c + 1], up),
        ))
    halo[1] += (
        remote(lat.at[1, 0, 0], x.at[1, 2, 0], h_s.at[4], h_r.at[4], down),
        remote(lat.at[1, 0, 1], x.at[1, 2, 5], h_s.at[5], h_r.at[5], up),
    )
    for both in halo:
        for copy in both:
            copy.start()

    def fold(i, carry):
        rows = pl.ds(pl.multiple_of(i * 64, 64), 64)
        by_row = [[raw2[b, e, rows].astype(F32) for e in range(3)] for b in range(3)]
        for p, u, picks in ((0, 0, (0,)), (0, 1, (1, 2)), (1, 0, (0, 1)), (1, 1, (2,))):
            taps = [functools.reduce(jnp.add, [by_row[b][e] for b in picks]) for e in range(3)]
            phase[p, u, rows, 0:CH] = taps[0].astype(BF16)
            phase[p, u, rows, CH : 2 * CH] = (taps[0] + taps[1] + taps[2]).astype(BF16)
            phase[p, u, rows, 2 * CH : 3 * CH] = taps[2].astype(BF16)
        return carry

    for copy in sums_a:
        copy.wait_recv()
    part = gath[0]
    for d in range(1, n_t):
        part = part + gath[d]
    pair[0] = part
    sums_b = [remote(pair.at[0], pair.at[d], p_s.at[d], p_r.at[d], row_peers[d]) for d in range(1, n_s)]
    for copy in sums_b:
        copy.start()

    w2_copy.wait()
    lax.fori_loop(0, CH // 64, fold, 0)

    corner = {}
    for c, f in UNITS:
        slot = c * 4 + f * 2
        if c == 0:
            rows = ((x.at[c, f, 3], x.at[c, f, 1]), (x.at[c, f, 2], x.at[c, f, 4]))
        else:
            rows = tuple((x.at[c, f, pl.ds(2, 2)], x.at[c, f, pl.ds(start, 2)]) for start in (0, 4))
        corner[c, f] = (
            remote(*rows[0], c_s.at[slot], c_r.at[slot], down),
            remote(*rows[1], c_s.at[slot + 1], c_r.at[slot + 1], up),
        )

    def forward(unit):
        @pl.when(t_me > 0)
        def _():
            z_copies[unit].wait_recv()
            for copy in corner[unit]:
                copy.start()

    forward(UNITS[0])

    for copy in sums_b:
        copy.wait_recv()
    total = pair[0]
    for d in range(1, n_s):
        total = total + pair[d]
    lane = lax.broadcasted_iota(jnp.int32, (1, 128), 1)
    second_clip = lax.rem(lane // 32, 2) == 1
    number = [(counts[c] * (cells * GROUP)).astype(F32) for c in range(2)]
    ratio = total / jnp.where(second_clip, number[1], number[0])
    mean = pltpu.roll(ratio, 64, 1)
    packed = jnp.where(lane < 64, ratio, lax.rsqrt(jnp.where(lane < 64, 0.0, ratio - mean * mean) + EPS))
    coef[...] = exact_dot(jnp.where(diagonal, packed, 0.0), membership((128, CH), 1))

    def activate(c, f, first=1, end=5):
        there = present(c, 2 * t_me - 2 + f)

        def row(r, carry):
            inside = jnp.where(((r < 2) & (s_me == 0)) | ((r > 3) & (s_me == n_s - 1)), 0.0, there)
            half = (x[c, f, r].astype(F32) - coef[c : c + 1]) * (coef[2 + c : 3 + c] * gain[...].reshape(1, CH) * 0.5) + nbias[...].reshape(1, CH) * 0.5
            act[c, f, r] = ((half + half * jnp.tanh(half)) * inside).astype(BF16)
            return carry

        lax.fori_loop(first, end, row, 0)

    def column(v):
        return lax.rem(lax.broadcasted_iota(jnp.int32, v.shape, 0), COLS)

    def before(v):
        return jnp.where(column(v) > 0, pltpu.roll(v, 1, 0), 0.0)

    def after(v):
        return jnp.where(column(v) < COLS - 1, pltpu.roll(v, v.shape[0] - 1, 0), 0.0)

    OWN, WIDE = (2, 3), (1, 2, 3, 4)

    def volume(c, frames, taps, rows=OWN):
        lhs = jnp.concatenate(
            [jnp.concatenate([act[c, f, r - 1 + b] for f in frames for b in range(3)], axis=1) for r in rows], axis=0
        )
        rhs = wide[pl.ds(taps[0], len(taps))].reshape(len(taps) * 3 * CH, 3 * CH)
        prod = dot(lhs, rhs)
        return before(prod[:, 0:CH]) + prod[:, CH : 2 * CH] + after(prod[:, 2 * CH :])

    def finish(c, f, rows=OWN):
        kept = present(c, 2 * t_me + f)
        resid = jnp.concatenate([x[c, 2 + f, r] for r in rows], axis=0).astype(F32)
        sums = last[...] if rows is WIDE else acc[c, f]
        value = ((resid + sums + b3[...].reshape(1, CH)) * kept).astype(BF16)
        for i, r in enumerate(rows):
            mid[c, f, r - 1] = value[i * COLS : (i + 1) * COLS]

    mid_copies = [
        (
            remote(mid.at[0, :, 2], mid.at[0, :, 0], m_s.at[0], m_r.at[0], down),
            remote(mid.at[0, :, 1], mid.at[0, :, 3], m_s.at[1], m_r.at[1], up),
        ),
        (
            remote(mid.at[1, 1, 2], mid.at[1, 1, 0], m_s.at[2], m_r.at[2], down),
            remote(mid.at[1, 1, 1], mid.at[1, 1, 3], m_s.at[3], m_r.at[3], up),
        ),
    ]

    stored = [
        pltpu.make_async_copy(ready.at[i // 4, :, i % 4], out.at[i // 4, :, i % 4], o_s.at[i]) for i in range(8)
    ]

    def emit(c, p, r, first_row):
        lhs = jnp.concatenate([jnp.concatenate([mid[c, f, first_row], mid[c, f, first_row + 1]], axis=1) for f in range(2)], axis=0)
        prod = dot(lhs, phase[p].reshape(2 * CH, 3 * CH))
        left, centre, right = prod[:, 0:CH], prod[:, CH : 2 * CH], prod[:, 2 * CH :]
        centre = centre + b2[...].reshape(1, CH)
        even = centre + (before(left) - left)
        odd = centre + (after(right) - right)
        for f in range(2):
            kept = present(c, 2 * t_me + f)
            for lane in range(CH // 128):
                cut = slice(lane * 128, lane * 128 + 128)
                rows = slice(f * COLS, (f + 1) * COLS)
                inter[f, lane, pl.ds(0, COLS, stride=2)] = even[rows, cut] * kept
                inter[f, lane, pl.ds(1, COLS, stride=2)] = odd[rows, cut] * kept
                ready[c, f, 2 * r + p, :, cut] = inter[f, lane].astype(BF16)
        stored[c * 4 + 2 * r + p].start()

    def inner(c):
        emit(c, 1, 0, 1)
        emit(c, 0, 1, 1)

    def outer(c):
        for copy in mid_copies[c]:
            copy.wait_recv()

        @pl.when(s_me == 0)
        def _():
            mid[c, :, 0] = jnp.zeros((2, COLS, CH), BF16)

        @pl.when(s_me == n_s - 1)
        def _():
            mid[c, :, 3] = jnp.zeros((2, COLS, CH), BF16)

        emit(c, 0, 0, 0)
        emit(c, 1, 1, 2)

    def arrived(unit):
        for copy in corner[unit]:
            copy.wait_recv()

    for copy in halo[0]:
        copy.wait_recv()
    activate(0, 2)
    activate(0, 3)
    forward(UNITS[1])
    for copy in w3_copies:
        copy.wait()
    acc[0, 0] = volume(0, (2,), (2,))
    acc[0, 1] = volume(0, (2, 3), (1, 2))
    for copy in halo[1]:
        copy.wait_recv()
    activate(1, 2, 0, 6)
    activate(1, 3)
    forward(UNITS[2])
    last[...] = volume(1, (2,), (2,), WIDE)
    acc[1, 1] = volume(1, (2, 3), (1, 2))
    forward(UNITS[3])

    @pl.when(t_me > 0)
    def _():
        arrived((0, 1))
        activate(0, 1)
        arrived((0, 0))
        activate(0, 0)
        acc[0, 1] += volume(0, (1,), (0,))
        acc[0, 0] += volume(0, (0, 1), (0, 1))

    finish(0, 0)
    finish(0, 1)
    for copy in mid_copies[0]:
        copy.start()

    @pl.when(t_me > 0)
    def _():
        arrived((1, 1))
        activate(1, 1, 0, 6)
        acc[1, 1] += volume(1, (1,), (0,))

    finish(1, 1)
    for copy in mid_copies[1]:
        copy.start()

    @pl.when(t_me > 0)
    def _():
        last[...] += volume(1, (1,), (1,), WIDE)

    inner(0)

    @pl.when(t_me > 0)
    def _():
        arrived((1, 0))
        activate(1, 0, 0, 6)
        last[...] += volume(1, (0,), (0,), WIDE)

    finish(1, 0, WIDE)
    outer(0)
    inner(1)
    outer(1)

    for copy in stored:
        copy.wait()

    for copy in sums_a + sums_b + [copy for both in halo + mid_copies for copy in both]:
        copy.wait_send()

    @pl.when(t_me < n_t - 1)
    def _():
        for unit in UNITS:
            z_copies[unit].wait_send()

    @pl.when(t_me > 0)
    def _():
        for unit in UNITS:
            for copy in corner[unit]:
                copy.wait_send()


def pass_on(given, out, held, i_s, o_s):
    part = lambda ref, i: ref.at[i // 4, i // 2 % 2, pl.ds(i % 2 * 2, 2)]
    loads = [pltpu.make_async_copy(part(given, i), part(held, i), i_s.at[i]) for i in range(8)]
    stores = [pltpu.make_async_copy(part(held, i), part(out, i), o_s.at[i]) for i in range(8)]
    for load in loads:
        load.start()
    for load, store in zip(loads, stores):
        load.wait()
        store.start()
    for store in stores:
        store.wait()


def body(latents, frame_counts, norm_gain, norm_bias, conv3_weight, conv3_bias, conv2_weight, conv2_bias):
    rows = latents.shape[2] * lax.axis_size("space")
    hbm, vmem, smem = (pl.BlockSpec(memory_space=space) for space in (pltpu.HBM, pltpu.VMEM, pltpu.SMEM))
    dma = pltpu.SemaphoreType.DMA
    decoded = pl.pallas_call(
        functools.partial(kernel, rows * COLS),
        out_shape=jax.ShapeDtypeStruct((2, 2, 4, 2 * COLS, CH), BF16),
        in_specs=[hbm, smem, vmem, vmem, hbm, vmem, hbm, vmem],
        out_specs=hbm,
        scratch_shapes=[
            pltpu.VMEM((2, 4, 6, COLS, CH), BF16),
            pltpu.VMEM((2, 4, 6, COLS, CH), BF16),
            pltpu.VMEM((3, 3, CH, 3 * CH), BF16),
            pltpu.VMEM((3, 3, CH, CH), BF16),
            pltpu.VMEM((2, 2, CH, 3 * CH), BF16),
            pltpu.VMEM((2, 2, 2 * COLS, CH), F32),
            pltpu.VMEM((2, 2, 4, COLS, CH), BF16),
            pltpu.VMEM((8, 1, 128), F32),
            pltpu.VMEM((4, 1, 128), F32),
            pltpu.VMEM((2, 3, 2 * COLS, 128), F32),
            pltpu.VMEM((8, CH), F32),
            pltpu.VMEM((2, 2, 4, 2 * COLS, CH), BF16),
            pltpu.VMEM((4 * COLS, CH), F32),
            dma, dma((9,)), dma, dma((8,)), dma((8,)), dma((4,)), dma((4,)),
            dma((4,)), dma((4,)), dma((8,)), dma((8,)), dma((8,)), dma((8,)), dma((4,)), dma((4,)), dma((8,)),
        ],
        compiler_params=pltpu.CompilerParams(collective_id=0, has_side_effects=True, vmem_limit_bytes=58 * 2**20),
        cost_estimate=pl.CostEstimate(flops=7 * 10**9, bytes_accessed=13 * 10**6, transcendentals=10**6),
    )(latents, frame_counts, norm_gain, norm_bias, conv3_weight, conv3_bias, conv2_weight, conv2_bias)
    return pl.pallas_call(
        pass_on,
        out_shape=jax.ShapeDtypeStruct(decoded.shape, BF16),
        in_specs=[hbm],
        out_specs=hbm,
        scratch_shapes=[pltpu.VMEM(decoded.shape, BF16), dma((8,)), dma((8,))],
        compiler_params=pltpu.CompilerParams(vmem_limit_bytes=58 * 2**20),
    )(decoded)


def solution(mesh):
    placed = (P("clip", "tm", "space", None, None), P("clip"), P(), P(), P(), P(), P(), P())
    return jax.shard_map(
        body, mesh=mesh, in_specs=placed, out_specs=P("clip", "tm", "space", None, None), check_vma=False
    )
```

```python
import functools

import jax
import jax.numpy as jnp
from jax import lax
from jax.experimental import pallas as pl
from jax.experimental.pallas import tpu as pltpu
from jax.sharding import PartitionSpec as P

MESH = pl.DeviceIdType.MESH
EPS = 1e-05
CH = 384
GROUP = 12
COLS = 64
F32 = jnp.float32
BF16 = jnp.bfloat16
UNITS = ((0, 1), (0, 0), (1, 1), (1, 0))


def dot(a, b):
    return jnp.dot(a, b, preferred_element_type=F32)


def exact_dot(a, onehot):
    high = a.astype(BF16)
    rest = a - high.astype(F32)
    middle = rest.astype(BF16)
    low = (rest - middle.astype(F32)).astype(BF16)
    parts = dot(jnp.concatenate([high.astype(F32), middle.astype(F32), low.astype(F32)], axis=0).astype(BF16), onehot)
    return parts[0:8] + parts[8:16] + parts[16:24]


def membership(shape, channel_axis):
    channel = lax.broadcasted_iota(jnp.int32, shape, channel_axis)
    first = lax.rem(lax.broadcasted_iota(jnp.int32, shape, 1 - channel_axis), 32) * GROUP
    return jnp.where((channel >= first) & (channel < first + GROUP), 1.0, 0.0).astype(BF16)


def kernel(
    cells, lat, counts, gain, nbias, w3, b3, w2, b2, out,
    x, act, wide, raw2, phase, acc, mid, pair, gath, inter, coef, ready, last,
    lsem, wsem, w2sem, p_s, p_r, g_s, g_r, z_s, z_r, h_s, h_r, c_s, c_r, m_s, m_r, o_s,
):
    n_t, n_s = lax.axis_size("tm"), lax.axis_size("space")
    t_me, s_me = lax.axis_index("tm"), lax.axis_index("space")
    later = {"tm": lax.rem(t_me + 1, n_t)}
    up, down = {"space": lax.rem(s_me + n_s - 1, n_s)}, {"space": lax.rem(s_me + 1, n_s)}

    def remote(src, dst, send, recv, device):
        return pltpu.make_async_remote_copy(
            src_ref=src, dst_ref=dst, send_sem=send, recv_sem=recv, device_id=device, device_id_type=MESH
        )

    own = pltpu.make_async_copy(lat, x.at[:, pl.ds(2, 2), pl.ds(2, 2)], lsem)
    own.start()

    column_peers = [{"tm": lax.rem(t_me + d, n_t)} for d in range(n_t)]
    row_peers = [{"space": lax.rem(s_me + d, n_s)} for d in range(n_s)]
    peers = column_peers[1:] + row_peers[1:]
    barrier = pltpu.get_barrier_semaphore()
    for peer in peers:
        pl.semaphore_signal(barrier, inc=1, device_id=peer, device_id_type=MESH)

    w2_copy = pltpu.make_async_copy(w2, raw2, w2sem)
    w2_copy.start()
    w3_copies = [
        pltpu.make_async_copy(w3.at[a, :, e], wide.at[a, :, :, pl.ds(e * CH, CH)], wsem.at[a * 3 + e])
        for a in (2, 1, 0)
        for e in range(3)
    ]
    for copy in w3_copies:
        copy.start()

    def present(c, frame):
        return (frame < counts[c]).astype(F32)

    own.wait()
    firsts, seconds = [], []
    for c in range(2):
        first = jnp.zeros((8, CH), F32)
        second = jnp.zeros((8, CH), F32)
        for f in range(2):
            f1 = jnp.zeros((8, CH), F32)
            f2 = jnp.zeros((8, CH), F32)
            for r in range(2):
                v = x[c, 2 + f, 2 + r].astype(F32).reshape(8, 8, CH)
                f1 += jnp.sum(v, axis=0)
                f2 += jnp.sum(v * v, axis=0)
            there = present(c, 2 * t_me + f)
            first += f1 * there
            second += f2 * there
        firsts.append(jnp.sum(first, axis=0, keepdims=True))
        seconds.append(jnp.sum(second, axis=0, keepdims=True))
    sums = jnp.concatenate(firsts + seconds + [jnp.zeros((4, CH), F32)], axis=0)
    grouped = exact_dot(sums, membership((CH, 128), 0))
    lane_row = lax.broadcasted_iota(jnp.int32, (8, 128), 1) // 32
    diagonal = lane_row == lax.broadcasted_iota(jnp.int32, (8, 128), 0)
    gath[0] = jnp.sum(jnp.where(diagonal, grouped, 0.0), axis=0, keepdims=True)

    pl.semaphore_wait(barrier, len(peers))

    sums_a = [remote(gath.at[0], gath.at[d], g_s.at[d], g_r.at[d], column_peers[d]) for d in range(1, n_t)]
    for copy in sums_a:
        copy.start()
    z_copies = {
        (c, f): remote(lat.at[c, f], x.at[c, f, pl.ds(2, 2)], z_s.at[c * 2 + f], z_r.at[c * 2 + f], later)
        for c, f in UNITS
    }

    @pl.when(t_me < n_t - 1)
    def _():
        for unit in UNITS:
            z_copies[unit].start()

    halo = []
    for c in range(2):
        halo.append((
            remote(lat.at[c, :, 1], x.at[c, pl.ds(2, 2), 1], h_s.at[2 * c], h_r.at[2 * c], down),
            remote(lat.at[c, :, 0], x.at[c, pl.ds(2, 2), 4], h_s.at[2 * c + 1], h_r.at[2 * c + 1], up),
        ))
    halo[1] += (
        remote(lat.at[1, 0, 0], x.at[1, 2, 0], h_s.at[4], h_r.at[4], down),
        remote(lat.at[1, 0, 1], x.at[1, 2, 5], h_s.at[5], h_r.at[5], up),
    )
    for both in halo:
        for copy in both:
            copy.start()

    def fold(i, carry):
        rows = pl.ds(pl.multiple_of(i * 64, 64), 64)
        by_row = [[raw2[b, e, rows].astype(F32) for e in range(3)] for b in range(3)]
        for p, u, picks in ((0, 0, (0,)), (0, 1, (1, 2)), (1, 0, (0, 1)), (1, 1, (2,))):
            taps = [functools.reduce(jnp.add, [by_row[b][e] for b in picks]) for e in range(3)]
            phase[p, u, rows, 0:CH] = taps[0].astype(BF16)
            phase[p, u, rows, CH : 2 * CH] = (taps[0] + taps[1] + taps[2]).astype(BF16)
            phase[p, u, rows, 2 * CH : 3 * CH] = taps[2].astype(BF16)
        return carry

    for copy in sums_a:
        copy.wait_recv()
    part = gath[0]
    for d in range(1, n_t):
        part = part + gath[d]
    pair[0] = part
    sums_b = [remote(pair.at[0], pair.at[d], p_s.at[d], p_r.at[d], row_peers[d]) for d in range(1, n_s)]
    for copy in sums_b:
        copy.start()

    w2_copy.wait()
    lax.fori_loop(0, CH // 64, fold, 0)

    corner = {}
    for c, f in UNITS:
        slot = c * 4 + f * 2
        if c == 0:
            rows = ((x.at[c, f, 3], x.at[c, f, 1]), (x.at[c, f, 2], x.at[c, f, 4]))
        else:
            rows = tuple((x.at[c, f, pl.ds(2, 2)], x.at[c, f, pl.ds(start, 2)]) for start in (0, 4))
        corner[c, f] = (
            remote(*rows[0], c_s.at[slot], c_r.at[slot], down),
            remote(*rows[1], c_s.at[slot + 1], c_r.at[slot + 1], up),
        )

    def forward(unit):
        @pl.when(t_me > 0)
        def _():
            z_copies[unit].wait_recv()
            for copy in corner[unit]:
                copy.start()

    forward(UNITS[0])

    for copy in sums_b:
        copy.wait_recv()
    total = pair[0]
    for d in range(1, n_s):
        total = total + pair[d]
    lane = lax.broadcasted_iota(jnp.int32, (1, 128), 1)
    second_clip = lax.rem(lane // 32, 2) == 1
    number = [(counts[c] * (cells * GROUP)).astype(F32) for c in range(2)]
    ratio = total / jnp.where(second_clip, number[1], number[0])
    mean = pltpu.roll(ratio, 64, 1)
    packed = jnp.where(lane < 64, ratio, lax.rsqrt(jnp.where(lane < 64, 0.0, ratio - mean * mean) + EPS))
    coef[...] = exact_dot(jnp.where(diagonal, packed, 0.0), membership((128, CH), 1))

    def activate(c, f, first=1, end=5):
        there = present(c, 2 * t_me - 2 + f)

        def row(r, carry):
            inside = jnp.where(((r < 2) & (s_me == 0)) | ((r > 3) & (s_me == n_s - 1)), 0.0, there)
            half = (x[c, f, r].astype(F32) - coef[c : c + 1]) * (coef[2 + c : 3 + c] * gain[...].reshape(1, CH) * 0.5) + nbias[...].reshape(1, CH) * 0.5
            act[c, f, r] = ((half + half * jnp.tanh(half)) * inside).astype(BF16)
            return carry

        lax.fori_loop(first, end, row, 0)

    def column(v):
        return lax.rem(lax.broadcasted_iota(jnp.int32, v.shape, 0), COLS)

    def before(v):
        return jnp.where(column(v) > 0, pltpu.roll(v, 1, 0), 0.0)

    def after(v):
        return jnp.where(column(v) < COLS - 1, pltpu.roll(v, v.shape[0] - 1, 0), 0.0)

    OWN, WIDE = (2, 3), (1, 2, 3, 4)

    def volume(parts, taps):
        lhs = jnp.concatenate(
            [
                jnp.concatenate([act[c, f, r - 1 + b] for f in frames for b in range(3)], axis=1)
                for c, frames, rows in parts
                for r in rows
            ],
            axis=0,
        )
        rhs = wide[pl.ds(taps[0], len(taps))].reshape(len(taps) * 3 * CH, 3 * CH)
        prod = dot(lhs, rhs)
        return before(prod[:, 0:CH]) + prod[:, CH : 2 * CH] + after(prod[:, 2 * CH :])

    def finish(c, f, rows=OWN):
        kept = present(c, 2 * t_me + f)
        resid = jnp.concatenate([x[c, 2 + f, r] for r in rows], axis=0).astype(F32)
        sums = last[...] if rows is WIDE else acc[c, f]
        value = ((resid + sums + b3[...].reshape(1, CH)) * kept).astype(BF16)
        for i, r in enumerate(rows):
            mid[c, f, r - 1] = value[i * COLS : (i + 1) * COLS]

    mid_copies = [
        (
            remote(mid.at[0, :, 2], mid.at[0, :, 0], m_s.at[0], m_r.at[0], down),
            remote(mid.at[0, :, 1], mid.at[0, :, 3], m_s.at[1], m_r.at[1], up),
        ),
        (
            remote(mid.at[1, 1, 2], mid.at[1, 1, 0], m_s.at[2], m_r.at[2], down),
            remote(mid.at[1, 1, 1], mid.at[1, 1, 3], m_s.at[3], m_r.at[3], up),
        ),
    ]

    stored = [
        pltpu.make_async_copy(ready.at[i // 4, :, i % 4], out.at[i // 4, :, i % 4], o_s.at[i]) for i in range(8)
    ]

    def emit(c, p, picks=(0, 1)):
        lhs = jnp.concatenate(
            [
                jnp.concatenate([mid[c, f, r + p], mid[c, f, r + p + 1]], axis=1)
                for r in picks
                for f in range(2)
            ],
            axis=0,
        )
        prod = dot(lhs, phase[p].reshape(2 * CH, 3 * CH))
        left, centre, right = prod[:, 0:CH], prod[:, CH : 2 * CH], prod[:, 2 * CH :]
        centre = centre + b2[...].reshape(1, CH)
        even = centre + (before(left) - left)
        odd = centre + (after(right) - right)
        for i, r in enumerate(picks):
            for f in range(2):
                kept = present(c, 2 * t_me + f)
                rows = slice((2 * i + f) * COLS, (2 * i + f + 1) * COLS)
                for lane in range(CH // 128):
                    cut = slice(lane * 128, lane * 128 + 128)
                    inter[f, lane, pl.ds(0, COLS, stride=2)] = even[rows, cut] * kept
                    inter[f, lane, pl.ds(1, COLS, stride=2)] = odd[rows, cut] * kept
                    ready[c, f, 2 * r + p, :, cut] = inter[f, lane].astype(BF16)
            stored[c * 4 + 2 * r + p].start()

    def decode(c):
        for copy in mid_copies[c]:
            copy.wait_recv()

        @pl.when(s_me == 0)
        def _():
            mid[c, :, 0] = jnp.zeros((2, COLS, CH), BF16)

        @pl.when(s_me == n_s - 1)
        def _():
            mid[c, :, 3] = jnp.zeros((2, COLS, CH), BF16)

        if c == 0:
            emit(c, 0, (0,))
            emit(c, 1, (1,))
        else:
            emit(c, 0)
            emit(c, 1)

    def arrived(unit):
        for copy in corner[unit]:
            copy.wait_recv()

    for both in halo:
        for copy in both:
            copy.wait_recv()
    activate(0, 2)
    activate(0, 3)
    forward(UNITS[1])
    activate(1, 2, 0, 6)
    activate(1, 3)
    for copy in w3_copies:
        copy.wait()
    value = volume(((0, (2, 3), OWN), (1, (2, 3), OWN)), (1, 2))
    acc[0, 1] = value[: 2 * COLS]
    acc[1, 1] = value[2 * COLS :]
    forward(UNITS[2])
    value = volume(((0, (2,), OWN), (1, (2,), WIDE)), (2,))
    acc[0, 0] = value[: 2 * COLS]
    last[...] = value[2 * COLS :]
    forward(UNITS[3])

    @pl.when(t_me > 0)
    def _():
        arrived((0, 1))
        activate(0, 1)
        arrived((0, 0))
        activate(0, 0)
        acc[0, 1] += volume(((0, (1,), OWN),), (0,))
        acc[0, 0] += volume(((0, (0, 1), OWN),), (0, 1))

    finish(0, 0)
    finish(0, 1)
    for copy in mid_copies[0]:
        copy.start()

    @pl.when(t_me > 0)
    def _():
        arrived((1, 1))
        activate(1, 1, 0, 6)
        acc[1, 1] += volume(((1, (1,), OWN),), (0,))

    finish(1, 1)
    for copy in mid_copies[1]:
        copy.start()

    @pl.when(t_me > 0)
    def _():
        last[...] += volume(((1, (1,), WIDE),), (1,))


    emit(0, 1, (0,))
    emit(0, 0, (1,))

    @pl.when(t_me > 0)
    def _():
        arrived((1, 0))
        activate(1, 0, 0, 6)
        last[...] += volume(((1, (0,), WIDE),), (0,))

    finish(1, 0, WIDE)
    decode(0)
    decode(1)

    for copy in stored:
        copy.wait()

    for copy in sums_a + sums_b + [copy for both in halo + mid_copies for copy in both]:
        copy.wait_send()

    @pl.when(t_me < n_t - 1)
    def _():
        for unit in UNITS:
            z_copies[unit].wait_send()

    @pl.when(t_me > 0)
    def _():
        for unit in UNITS:
            for copy in corner[unit]:
                copy.wait_send()


def pass_on(given, out, held, i_s, o_s):
    part = lambda ref, i: ref.at[i // 2, i % 2]
    loads = [pltpu.make_async_copy(part(given, i), part(held, i), i_s.at[i]) for i in range(4)]
    stores = [pltpu.make_async_copy(part(held, i), part(out, i), o_s.at[i]) for i in range(4)]
    for load in loads:
        load.start()
    for load, store in zip(loads, stores):
        load.wait()
        store.start()
    for store in stores:
        store.wait()


def body(latents, frame_counts, norm_gain, norm_bias, conv3_weight, conv3_bias, conv2_weight, conv2_bias):
    rows = latents.shape[2] * lax.axis_size("space")
    hbm, vmem, smem = (pl.BlockSpec(memory_space=space) for space in (pltpu.HBM, pltpu.VMEM, pltpu.SMEM))
    dma = pltpu.SemaphoreType.DMA
    decoded = pl.pallas_call(
        functools.partial(kernel, rows * COLS),
        out_shape=jax.ShapeDtypeStruct((2, 2, 4, 2 * COLS, CH), BF16),
        in_specs=[hbm, smem, vmem, vmem, hbm, vmem, hbm, vmem],
        out_specs=hbm,
        scratch_shapes=[
            pltpu.VMEM((2, 4, 6, COLS, CH), BF16),
            pltpu.VMEM((2, 4, 6, COLS, CH), BF16),
            pltpu.VMEM((3, 3, CH, 3 * CH), BF16),
            pltpu.VMEM((3, 3, CH, CH), BF16),
            pltpu.VMEM((2, 2, CH, 3 * CH), BF16),
            pltpu.VMEM((2, 2, 2 * COLS, CH), F32),
            pltpu.VMEM((2, 2, 4, COLS, CH), BF16),
            pltpu.VMEM((8, 1, 128), F32),
            pltpu.VMEM((4, 1, 128), F32),
            pltpu.VMEM((2, 3, 2 * COLS, 128), F32),
            pltpu.VMEM((8, CH), F32),
            pltpu.VMEM((2, 2, 4, 2 * COLS, CH), BF16),
            pltpu.VMEM((4 * COLS, CH), F32),
            dma, dma((9,)), dma, dma((8,)), dma((8,)), dma((4,)), dma((4,)),
            dma((4,)), dma((4,)), dma((8,)), dma((8,)), dma((8,)), dma((8,)), dma((4,)), dma((4,)), dma((8,)),
        ],
        compiler_params=pltpu.CompilerParams(collective_id=0, has_side_effects=True, vmem_limit_bytes=58 * 2**20),
        cost_estimate=pl.CostEstimate(flops=7 * 10**9, bytes_accessed=13 * 10**6, transcendentals=10**6),
    )(latents, frame_counts, norm_gain, norm_bias, conv3_weight, conv3_bias, conv2_weight, conv2_bias)
    return pl.pallas_call(
        pass_on,
        out_shape=jax.ShapeDtypeStruct(decoded.shape, BF16),
        in_specs=[hbm],
        out_specs=hbm,
        scratch_shapes=[pltpu.VMEM(decoded.shape, BF16), dma((4,)), dma((4,))],
        compiler_params=pltpu.CompilerParams(vmem_limit_bytes=58 * 2**20),
    )(decoded)


def solution(mesh):
    placed = (P("clip", "tm", "space", None, None), P("clip"), P(), P(), P(), P(), P(), P())
    return jax.shard_map(
        body, mesh=mesh, in_specs=placed, out_specs=P("clip", "tm", "space", None, None), check_vma=False
    )
```

```python
import functools

import jax
import jax.numpy as jnp
from jax import lax
from jax.experimental import pallas as pl
from jax.experimental.pallas import tpu as pltpu
from jax.sharding import PartitionSpec as P

MESH = pl.DeviceIdType.MESH
EPS = 1e-05
CH = 384
GROUP = 12
COLS = 64
F32 = jnp.float32
BF16 = jnp.bfloat16
UNITS = ((0, 1), (0, 0), (1, 1), (1, 0))


def dot(a, b):
    return jnp.dot(a, b, preferred_element_type=F32)


def exact_dot(a, onehot):
    high = a.astype(BF16)
    rest = a - high.astype(F32)
    middle = rest.astype(BF16)
    low = (rest - middle.astype(F32)).astype(BF16)
    parts = dot(jnp.concatenate([high.astype(F32), middle.astype(F32), low.astype(F32)], axis=0).astype(BF16), onehot)
    return parts[0:8] + parts[8:16] + parts[16:24]


def membership(shape, channel_axis):
    channel = lax.broadcasted_iota(jnp.int32, shape, channel_axis)
    first = lax.rem(lax.broadcasted_iota(jnp.int32, shape, 1 - channel_axis), 32) * GROUP
    return jnp.where((channel >= first) & (channel < first + GROUP), 1.0, 0.0).astype(BF16)


def kernel(
    cells, lat, counts, gain, nbias, w3, b3, w2, b2, out,
    x, act, wide, raw2, phase, acc, mid, pair, gath, inter, coef, ready, last,
    lsem, wsem, w2sem, p_s, p_r, g_s, g_r, z_s, z_r, h_s, h_r, c_s, c_r, m_s, m_r, o_s,
):
    n_t, n_s = lax.axis_size("tm"), lax.axis_size("space")
    t_me, s_me = lax.axis_index("tm"), lax.axis_index("space")
    later = {"tm": lax.rem(t_me + 1, n_t)}
    up, down = {"space": lax.rem(s_me + n_s - 1, n_s)}, {"space": lax.rem(s_me + 1, n_s)}

    def remote(src, dst, send, recv, device):
        return pltpu.make_async_remote_copy(
            src_ref=src, dst_ref=dst, send_sem=send, recv_sem=recv, device_id=device, device_id_type=MESH
        )

    own = pltpu.make_async_copy(lat, x.at[:, pl.ds(2, 2), pl.ds(2, 2)], lsem)
    own.start()

    column_peers = [{"tm": lax.rem(t_me + d, n_t)} for d in range(n_t)]
    row_peers = [{"space": lax.rem(s_me + d, n_s)} for d in range(n_s)]
    peers = column_peers[1:] + row_peers[1:]
    barrier = pltpu.get_barrier_semaphore()
    for peer in peers:
        pl.semaphore_signal(barrier, inc=1, device_id=peer, device_id_type=MESH)

    w2_copy = pltpu.make_async_copy(w2, raw2, w2sem)
    w2_copy.start()
    w3_copies = [
        pltpu.make_async_copy(w3.at[a, :, e], wide.at[a, :, :, pl.ds(e * CH, CH)], wsem.at[a * 3 + e])
        for a in (2, 1, 0)
        for e in range(3)
    ]
    for copy in w3_copies:
        copy.start()

    def present(c, frame):
        return (frame < counts[c]).astype(F32)

    own.wait()
    firsts, seconds = [], []
    for c in range(2):
        first = jnp.zeros((8, CH), F32)
        second = jnp.zeros((8, CH), F32)
        for f in range(2):
            f1 = jnp.zeros((8, CH), F32)
            f2 = jnp.zeros((8, CH), F32)
            for r in range(2):
                v = x[c, 2 + f, 2 + r].astype(F32).reshape(8, 8, CH)
                f1 += jnp.sum(v, axis=0)
                f2 += jnp.sum(v * v, axis=0)
            there = present(c, 2 * t_me + f)
            first += f1 * there
            second += f2 * there
        firsts.append(jnp.sum(first, axis=0, keepdims=True))
        seconds.append(jnp.sum(second, axis=0, keepdims=True))
    sums = jnp.concatenate(firsts + seconds + [jnp.zeros((4, CH), F32)], axis=0)
    grouped = exact_dot(sums, membership((CH, 128), 0))
    lane_row = lax.broadcasted_iota(jnp.int32, (8, 128), 1) // 32
    diagonal = lane_row == lax.broadcasted_iota(jnp.int32, (8, 128), 0)
    gath[0] = jnp.sum(jnp.where(diagonal, grouped, 0.0), axis=0, keepdims=True)

    pl.semaphore_wait(barrier, len(peers))

    sums_a = [remote(gath.at[0], gath.at[d], g_s.at[d], g_r.at[d], column_peers[d]) for d in range(1, n_t)]
    for copy in sums_a:
        copy.start()
    z_copies = {
        (c, f): remote(lat.at[c, f], x.at[c, f, pl.ds(2, 2)], z_s.at[c * 2 + f], z_r.at[c * 2 + f], later)
        for c, f in UNITS
    }

    @pl.when(t_me < n_t - 1)
    def _():
        for unit in UNITS:
            z_copies[unit].start()

    halo = []
    for c in range(2):
        halo.append((
            remote(lat.at[c, :, 1], x.at[c, pl.ds(2, 2), 1], h_s.at[2 * c], h_r.at[2 * c], down),
            remote(lat.at[c, :, 0], x.at[c, pl.ds(2, 2), 4], h_s.at[2 * c + 1], h_r.at[2 * c + 1], up),
        ))
    halo[1] += (
        remote(lat.at[1, 0, 0], x.at[1, 2, 0], h_s.at[4], h_r.at[4], down),
        remote(lat.at[1, 0, 1], x.at[1, 2, 5], h_s.at[5], h_r.at[5], up),
    )
    for both in halo:
        for copy in both:
            copy.start()

    def fold(i, carry):
        rows = pl.ds(pl.multiple_of(i * 64, 64), 64)
        by_row = [[raw2[b, e, rows].astype(F32) for e in range(3)] for b in range(3)]
        for p, u, picks in ((0, 0, (0,)), (0, 1, (1, 2)), (1, 0, (0, 1)), (1, 1, (2,))):
            taps = [functools.reduce(jnp.add, [by_row[b][e] for b in picks]) for e in range(3)]
            phase[p, u, rows, 0:CH] = taps[0].astype(BF16)
            phase[p, u, rows, CH : 2 * CH] = (taps[0] + taps[1] + taps[2]).astype(BF16)
            phase[p, u, rows, 2 * CH : 3 * CH] = taps[2].astype(BF16)
        return carry

    for copy in sums_a:
        copy.wait_recv()
    part = gath[0]
    for d in range(1, n_t):
        part = part + gath[d]
    pair[0] = part
    sums_b = [remote(pair.at[0], pair.at[d], p_s.at[d], p_r.at[d], row_peers[d]) for d in range(1, n_s)]
    for copy in sums_b:
        copy.start()

    w2_copy.wait()
    lax.fori_loop(0, CH // 64, fold, 0)

    corner = {}
    for c, f in UNITS:
        slot = c * 4 + f * 2
        if c == 0:
            rows = ((x.at[c, f, 3], x.at[c, f, 1]), (x.at[c, f, 2], x.at[c, f, 4]))
        else:
            rows = tuple((x.at[c, f, pl.ds(2, 2)], x.at[c, f, pl.ds(start, 2)]) for start in (0, 4))
        corner[c, f] = (
            remote(*rows[0], c_s.at[slot], c_r.at[slot], down),
            remote(*rows[1], c_s.at[slot + 1], c_r.at[slot + 1], up),
        )

    def forward(unit):
        @pl.when(t_me > 0)
        def _():
            z_copies[unit].wait_recv()
            for copy in corner[unit]:
                copy.start()

    forward(UNITS[0])

    for copy in sums_b:
        copy.wait_recv()
    total = pair[0]
    for d in range(1, n_s):
        total = total + pair[d]
    lane = lax.broadcasted_iota(jnp.int32, (1, 128), 1)
    second_clip = lax.rem(lane // 32, 2) == 1
    number = [(counts[c] * (cells * GROUP)).astype(F32) for c in range(2)]
    ratio = total / jnp.where(second_clip, number[1], number[0])
    mean = pltpu.roll(ratio, 64, 1)
    packed = jnp.where(lane < 64, ratio, lax.rsqrt(jnp.where(lane < 64, 0.0, ratio - mean * mean) + EPS))
    coef[...] = exact_dot(jnp.where(diagonal, packed, 0.0), membership((128, CH), 1))

    def activate(c, f, first=1, end=5):
        there = present(c, 2 * t_me - 2 + f)

        def row(r, carry):
            inside = jnp.where(((r < 2) & (s_me == 0)) | ((r > 3) & (s_me == n_s - 1)), 0.0, there)
            half = (x[c, f, r].astype(F32) - coef[c : c + 1]) * (coef[2 + c : 3 + c] * gain[...].reshape(1, CH) * 0.5) + nbias[...].reshape(1, CH) * 0.5
            act[c, f, r] = ((half + half * jnp.tanh(half)) * inside).astype(BF16)
            return carry

        lax.fori_loop(first, end, row, 0)

    def column(v):
        return lax.rem(lax.broadcasted_iota(jnp.int32, v.shape, 0), COLS)

    def before(v):
        return jnp.where(column(v) > 0, pltpu.roll(v, 1, 0), 0.0)

    def after(v):
        return jnp.where(column(v) < COLS - 1, pltpu.roll(v, v.shape[0] - 1, 0), 0.0)

    OWN, WIDE = (2, 3), (1, 2, 3, 4)

    def volume(c, frames, taps, rows=OWN):
        lhs = jnp.concatenate(
            [jnp.concatenate([act[c, f, r - 1 + b] for f in frames for b in range(3)], axis=1) for r in rows], axis=0
        )
        rhs = wide[pl.ds(taps[0], len(taps))].reshape(len(taps) * 3 * CH, 3 * CH)
        prod = dot(lhs, rhs)
        return before(prod[:, 0:CH]) + prod[:, CH : 2 * CH] + after(prod[:, 2 * CH :])

    def finish(c, f, rows=OWN):
        kept = present(c, 2 * t_me + f)
        resid = jnp.concatenate([x[c, 2 + f, r] for r in rows], axis=0).astype(F32)
        sums = last[...] if rows is WIDE else acc[c, f]
        value = ((resid + sums + b3[...].reshape(1, CH)) * kept).astype(BF16)
        for i, r in enumerate(rows):
            mid[c, f, r - 1] = value[i * COLS : (i + 1) * COLS]

    mid_copies = [
        (
            remote(mid.at[0, :, 2], mid.at[0, :, 0], m_s.at[0], m_r.at[0], down),
            remote(mid.at[0, :, 1], mid.at[0, :, 3], m_s.at[1], m_r.at[1], up),
        ),
        (
            remote(mid.at[1, 1, 2], mid.at[1, 1, 0], m_s.at[2], m_r.at[2], down),
            remote(mid.at[1, 1, 1], mid.at[1, 1, 3], m_s.at[3], m_r.at[3], up),
        ),
    ]

    stored = [
        pltpu.make_async_copy(ready.at[i // 4, :, i % 4], out.at[i // 4, :, i % 4], o_s.at[i]) for i in range(8)
    ]

    def emit(c, p, r, first_row):
        lhs = jnp.concatenate([jnp.concatenate([mid[c, f, first_row], mid[c, f, first_row + 1]], axis=1) for f in range(2)], axis=0)
        prod = dot(lhs, phase[p].reshape(2 * CH, 3 * CH))
        left, centre, right = prod[:, 0:CH], prod[:, CH : 2 * CH], prod[:, 2 * CH :]
        centre = centre + b2[...].reshape(1, CH)
        even = centre + (before(left) - left)
        odd = centre + (after(right) - right)
        for f in range(2):
            kept = present(c, 2 * t_me + f)
            for lane in range(CH // 128):
                cut = slice(lane * 128, lane * 128 + 128)
                rows = slice(f * COLS, (f + 1) * COLS)
                inter[f, lane, pl.ds(0, COLS, stride=2)] = even[rows, cut] * kept
                inter[f, lane, pl.ds(1, COLS, stride=2)] = odd[rows, cut] * kept
                ready[c, f, 2 * r + p, :, cut] = inter[f, lane].astype(BF16)
        stored[c * 4 + 2 * r + p].start()

    def inner(c):
        emit(c, 1, 0, 1)
        emit(c, 0, 1, 1)

    def outer(c):
        for copy in mid_copies[c]:
            copy.wait_recv()

        @pl.when(s_me == 0)
        def _():
            mid[c, :, 0] = jnp.zeros((2, COLS, CH), BF16)

        @pl.when(s_me == n_s - 1)
        def _():
            mid[c, :, 3] = jnp.zeros((2, COLS, CH), BF16)

        emit(c, 0, 0, 0)
        emit(c, 1, 1, 2)

    def arrived(unit):
        for copy in corner[unit]:
            copy.wait_recv()

    for copy in halo[0]:
        copy.wait_recv()
    activate(0, 2)
    activate(0, 3)
    forward(UNITS[1])
    for copy in w3_copies:
        copy.wait()
    acc[0, 0] = volume(0, (2,), (2,))
    acc[0, 1] = volume(0, (2, 3), (1, 2))
    for copy in halo[1]:
        copy.wait_recv()
    activate(1, 2, 0, 6)
    activate(1, 3)
    forward(UNITS[2])
    last[...] = volume(1, (2,), (2,), WIDE)
    acc[1, 1] = volume(1, (2, 3), (1, 2))
    forward(UNITS[3])

    @pl.when(t_me > 0)
    def _():
        arrived((0, 1))
        activate(0, 1)
        arrived((0, 0))
        activate(0, 0)
        acc[0, 1] += volume(0, (1,), (0,))
        acc[0, 0] += volume(0, (0, 1), (0, 1))

    finish(0, 0)
    finish(0, 1)
    for copy in mid_copies[0]:
        copy.start()

    @pl.when(t_me > 0)
    def _():
        arrived((1, 1))
        activate(1, 1, 0, 6)
        acc[1, 1] += volume(1, (1,), (0,))

    finish(1, 1)
    for copy in mid_copies[1]:
        copy.start()

    @pl.when(t_me > 0)
    def _():
        last[...] += volume(1, (1,), (1,), WIDE)

    inner(0)

    @pl.when(t_me > 0)
    def _():
        arrived((1, 0))
        activate(1, 0, 0, 6)
        last[...] += volume(1, (0,), (0,), WIDE)

    finish(1, 0, WIDE)
    outer(0)
    inner(1)
    outer(1)

    for copy in stored:
        copy.wait()

    for copy in sums_a + sums_b + [copy for both in halo + mid_copies for copy in both]:
        copy.wait_send()

    @pl.when(t_me < n_t - 1)
    def _():
        for unit in UNITS:
            z_copies[unit].wait_send()

    @pl.when(t_me > 0)
    def _():
        for unit in UNITS:
            for copy in corner[unit]:
                copy.wait_send()


def pass_on(given, out, held, i_s, o_s):
    part = lambda ref, i: ref.at[i // 2, i % 2]
    loads = [pltpu.make_async_copy(part(given, i), part(held, i), i_s.at[i]) for i in range(4)]
    stores = [pltpu.make_async_copy(part(held, i), part(out, i), o_s.at[i]) for i in range(4)]
    for load in loads:
        load.start()
    for load, store in zip(loads, stores):
        load.wait()
        store.start()
    for store in stores:
        store.wait()


def body(latents, frame_counts, norm_gain, norm_bias, conv3_weight, conv3_bias, conv2_weight, conv2_bias):
    rows = latents.shape[2] * lax.axis_size("space")
    hbm, vmem, smem = (pl.BlockSpec(memory_space=space) for space in (pltpu.HBM, pltpu.VMEM, pltpu.SMEM))
    dma = pltpu.SemaphoreType.DMA
    decoded = pl.pallas_call(
        functools.partial(kernel, rows * COLS),
        out_shape=jax.ShapeDtypeStruct((2, 2, 4, 2 * COLS, CH), BF16),
        in_specs=[hbm, smem, vmem, vmem, hbm, vmem, hbm, vmem],
        out_specs=hbm,
        scratch_shapes=[
            pltpu.VMEM((2, 4, 6, COLS, CH), BF16),
            pltpu.VMEM((2, 4, 6, COLS, CH), BF16),
            pltpu.VMEM((3, 3, CH, 3 * CH), BF16),
            pltpu.VMEM((3, 3, CH, CH), BF16),
            pltpu.VMEM((2, 2, CH, 3 * CH), BF16),
            pltpu.VMEM((2, 2, 2 * COLS, CH), F32),
            pltpu.VMEM((2, 2, 4, COLS, CH), BF16),
            pltpu.VMEM((8, 1, 128), F32),
            pltpu.VMEM((4, 1, 128), F32),
            pltpu.VMEM((2, 3, 2 * COLS, 128), F32),
            pltpu.VMEM((8, CH), F32),
            pltpu.VMEM((2, 2, 4, 2 * COLS, CH), BF16),
            pltpu.VMEM((4 * COLS, CH), F32),
            dma, dma((9,)), dma, dma((8,)), dma((8,)), dma((4,)), dma((4,)),
            dma((4,)), dma((4,)), dma((8,)), dma((8,)), dma((8,)), dma((8,)), dma((4,)), dma((4,)), dma((8,)),
        ],
        compiler_params=pltpu.CompilerParams(collective_id=0, has_side_effects=True, vmem_limit_bytes=58 * 2**20),
        cost_estimate=pl.CostEstimate(flops=7 * 10**9, bytes_accessed=13 * 10**6, transcendentals=10**6),
    )(latents, frame_counts, norm_gain, norm_bias, conv3_weight, conv3_bias, conv2_weight, conv2_bias)
    return pl.pallas_call(
        pass_on,
        out_shape=jax.ShapeDtypeStruct(decoded.shape, BF16),
        in_specs=[hbm],
        out_specs=hbm,
        scratch_shapes=[pltpu.VMEM(decoded.shape, BF16), dma((4,)), dma((4,))],
        compiler_params=pltpu.CompilerParams(vmem_limit_bytes=58 * 2**20),
    )(decoded)


def solution(mesh):
    placed = (P("clip", "tm", "space", None, None), P("clip"), P(), P(), P(), P(), P(), P())
    return jax.shard_map(
        body, mesh=mesh, in_specs=placed, out_specs=P("clip", "tm", "space", None, None), check_vma=False
    )
```
